128 devices in a mesh: row: 8 (over x, y_hi), col: 16 (over y_lo, z, core).
Axes of the slice: x: 4, y: 4 (y_hi: 2, y_lo: 2; y = y_hi * 2 + y_lo), z: 4, core: 2. Of those that a mesh axis runs over, the one named last changes fastest.
Arguments:
- features: bfloat16 [65536, 256], P(('row', 'col')), may hold values from -4 to 4
- inject: bfloat16 [65536, 256], P(('row', 'col')), may hold values from -6 to 6
- weight: bfloat16 [256, 256], replicated, may hold values from -0.375 to 0.375
- tiles: bfloat16 [8, 16, 128, 256, 256], P('row', 'col'), may hold values from -0.046875 to 0.046875
- tile_rows: int32 [8, 16, 128], P('row', 'col'), may hold values from 0 to 31, as said below
- tile_cols: int32 [8, 16, 128], P('row', 'col'), may hold values from 0 to 15, as said below
- tile_count: int32 [8, 16], P('row', 'col'), may hold values from 32 to 128, as said below
- flags: int32 [256], P(('row', 'col')), may hold values 0 or 1
Outputs:
- states: bfloat16 [65536, 256], P(('row', 'col'))
- residual: float32 [256], P(('row', 'col'))
The draws below stay inside these ranges and needn't reach their ends.
Inputs may be any that keep to these rules, and one draw needn't show every extreme that they name: `tile_count`: at most 128 live tiles at a grid position, exactly 128 at position (0, 0). `tile_rows`: no two tile slots of one grid position share both block row and block column. `tile_cols`: no two tile slots of one grid position share both block row and block column.
All inputs are finite; a program needn't handle non-finite values. No bound on the sum of `flags` on one device may be relied on, other than what follows from the above.
Results may differ from the reference program's by a relative error of at most 0.014.
Values may be sent and summed in bfloat16 or wider, within the bound.
No kernel may reach another device: no remote copies, remote signals or barrier semaphores. Data moves between devices by JAX's collectives and lax.ppermute only.
A program may use at most 128 MiB of HBM per device.

```python
import jax
import jax.numpy as jnp
from jax import lax

F = 256
BS = 256
SB = 2
NT_DEV = 128
ITERS = 2
NB = 256
V = 65536
N_ROW = 8
N_COL = 16


def shared_pairs(key):
    total = N_COL * SB * N_ROW * SB
    keys = jax.random.split(jax.random.fold_in(key, 7), N_ROW * N_COL)
    picked = jax.vmap(lambda k: jax.random.permutation(k, total)[:NT_DEV])(keys)
    return picked.reshape(N_ROW, N_COL, NT_DEV).astype(jnp.int32)


def draw_tile_rows(key, part):
    pairs = shared_pairs(key)
    return (pairs // (N_ROW * SB)).astype(jnp.int32)


def draw_tile_cols(key, part):
    pairs = shared_pairs(key)
    return (pairs % (N_ROW * SB)).astype(jnp.int32)


def draw_tile_count(key, part):
    key = jax.random.fold_in(key, 11)
    counts = jax.random.randint(key, (N_ROW, N_COL), NT_DEV // 4, NT_DEV + 1)
    first = (jnp.arange(N_ROW)[:, None] == 0) & (jnp.arange(N_COL)[None, :] == 0)
    return jnp.where(first, NT_DEV, counts).astype(jnp.int32)


def touch_ends(array, rng, smallest, high):
    spot = [jax.random.randint(jax.random.fold_in(rng, axis), (), 0, length) for axis, length in enumerate(array.shape)]
    widest = array.shape.index(max(array.shape))
    next_to = spot[:widest] + [(spot[widest] + 1) % array.shape[widest]] + spot[widest + 1:]
    return array.at[tuple(spot)].set(smallest).at[tuple(next_to)].set(high)


def block_levels(key, dims, cuts, smallest, top_value):
    def one(axis_at, parts):
        draws = jax.random.uniform(jax.random.fold_in(jax.random.fold_in(key, 6), axis_at), (parts,), jnp.float32, smallest / len(cuts), top_value / len(cuts))
        return jnp.repeat(jnp.exp(draws), dims[axis_at] // parts).reshape((-1,) + (1,) * (len(dims) - axis_at - 1))

    level = one(*cuts[0])
    for cut in cuts[1:]:
        level = level * one(*cut)
    return level


def gaussian(stream_key, extent, spread, reach, cuts=(), held_as=jnp.bfloat16):
    result = spread * jax.random.normal(stream_key, extent, jnp.float32)
    if cuts:
        result = result * block_levels(stream_key, extent, cuts, -0.22, 0.18)
    return jnp.clip(result, -reach, reach).astype(held_as)


def setup_inputs(seed: int = 0) -> dict:
    seeds = jax.random.split(jax.random.key(seed), 9)
    return {
        "features": gaussian(seeds[0], (V, F), 0.5, 4.0, ((0, 128),)),
        "inject": gaussian(seeds[1], (V, F), 1.0, 6.0, ((0, 128),)),
        "weight": gaussian(seeds[2], (F, F), F ** -0.5, 0.375),
        "tiles": gaussian(seeds[3], (N_ROW, N_COL, NT_DEV, BS, BS), (BS * NT_DEV // SB) ** -0.5, 0.046875, ((0, 8), (1, 16))),
        "tile_rows": draw_tile_rows(jax.random.fold_in(seeds[8], 71), 0),
        "tile_cols": draw_tile_cols(jax.random.fold_in(seeds[8], 71), 0),
        "tile_count": draw_tile_count(jax.random.fold_in(seeds[8], 71), 0),
        "flags": touch_ends((jax.random.randint(seeds[7], (NB,), 0, 4) < 1).astype(jnp.int32), jax.random.fold_in(seeds[7], 1), 0, 1),
    }


def device_partial(tile_set, rows_list, cols_list, count, column_group):
    start = jnp.zeros((N_COL * SB * BS, F), jnp.float32)

    def add_tile(t, acc):
        block = lax.dynamic_slice_in_dim(column_group, (cols_list[t] * BS).astype(jnp.int32), BS, 0)
        term = jnp.dot(tile_set[t], block, preferred_element_type=jnp.float32)
        where = (rows_list[t] * BS).astype(jnp.int32)
        current = lax.dynamic_slice_in_dim(acc, where, BS, 0)
        return lax.dynamic_update_slice_in_dim(acc, current + term, where, 0)

    return lax.fori_loop(jnp.int32(0), count.astype(jnp.int32), add_tile, start)


def reference(features, inject, weight, tiles, tile_rows, tile_cols, tile_count, flags):
    keep = jnp.repeat(flags, BS)[:, None] == 1
    state = features
    previous = features
    for step in range(ITERS):
        previous = state
        slabs = state.reshape(N_ROW, N_COL, SB * BS, F)

        def row_sum(r):
            def over_col(acc, c):
                column_group = slabs[:, c].reshape(N_ROW * SB * BS, F)
                part = device_partial(tiles[r, c], tile_rows[r, c], tile_cols[r, c], tile_count[r, c], column_group)
                rounded = lax.optimization_barrier(part.astype(jnp.bfloat16))
                return acc + rounded.astype(jnp.float32), None

            acc, unused = lax.scan(over_col, jnp.zeros((N_COL * SB * BS, F), jnp.float32), jnp.arange(N_COL, dtype=jnp.int32))
            return acc

        aggregate = lax.map(row_sum, jnp.arange(N_ROW, dtype=jnp.int32)).reshape(V, F).astype(jnp.bfloat16)
        pre = jnp.dot(aggregate, weight, preferred_element_type=jnp.float32) + inject.astype(jnp.float32)
        update = jnp.tanh(pre).astype(jnp.bfloat16)
        state = jnp.where(keep, state, update)
    change = state.astype(jnp.float32) - previous.astype(jnp.float32)
    residual = jnp.sum((change * change).reshape(NB, BS * F), axis=1)
    return state, residual
```

```python
import functools

import jax
import jax.numpy as jnp
from jax import lax
from jax.experimental import pallas as pl
from jax.experimental.pallas import tpu as pltpu
from jax.sharding import PartitionSpec as P

ITERS = 2
B = 256
BF = jnp.bfloat16
F32 = jnp.float32
N_SLOT = 32
UNROLL = 16
VMEM_LIMIT = 40 * 2**20


def col_perm(f):
    pairs = []
    for i in range(16):
        y, z, c = f(i // 8, i // 2 % 4, i % 2)
        pairs.append((i, (y % 2) * 8 + (z % 4) * 2 + c % 2))
    return pairs


def row_perm(f):
    pairs = []
    for i in range(8):
        x, y = f(i // 2, i % 2)
        pairs.append((i, (x % 4) * 2 + y % 2))
    return pairs


CORE = col_perm(lambda y, z, c: (y, z, c + 1))
Z_UP = col_perm(lambda y, z, c: (y, z + 1, c))
Z_DOWN = col_perm(lambda y, z, c: (y, z - 1, c))
Y_LO = col_perm(lambda y, z, c: (y + 1, z, c))
Y_HI = row_perm(lambda x, y: (x, y + 1))
X_UP = row_perm(lambda x, y: (x + 1, y))
X_DOWN = row_perm(lambda x, y: (x - 1, y))


def tile_words(rows, cols, count):
    row, col = lax.axis_index("row"), lax.axis_index("col")
    x, yh = row >> 1, row & 1
    yl, z, core = col >> 3, (col >> 1) & 3, col & 1
    half = ((rows >> 1) & 1) ^ core
    dst = (rows & 1) * 16 + half * 8 + (((rows >> 2) - z) & 3) * 2 + ((rows >> 4) ^ yl)
    src = (((cols >> 2) - x) & 3) * 4 + (((cols >> 1) & 1) ^ yh) * 2 + (cols & 1)
    live = jnp.arange(rows.shape[0], dtype=jnp.int32) < count
    return src + jnp.where(live, dst, N_SLOT) * 256


def tile_kernel(words, count, tiles, *refs):
    pieces, outs = refs[:16], refs[16:20]
    state, acc = refs[20:]
    acc[...] = jnp.zeros_like(acc)
    for s, piece in enumerate(pieces):
        state[s] = piece[...]

    @pl.loop(0, (count[0] + UNROLL - 1) // UNROLL)
    def _(i):
        for u in range(UNROLL):
            t = i * UNROLL + u
            word = words[t]
            acc[word >> 8] += jnp.dot(tiles[t], state[word & 255], preferred_element_type=F32)

    for i, out in enumerate(outs):
        for s in range(8):
            out[s] = acc[i * 8 + s].astype(BF)


def tile_sums(words, count, tiles, pieces):
    smem = pl.BlockSpec(memory_space=pltpu.SMEM)
    vmem = pl.BlockSpec(memory_space=pltpu.VMEM)
    out = jax.ShapeDtypeStruct((8, B, B), BF)
    return pl.pallas_call(
        tile_kernel,
        out_shape=(out,) * 4,
        in_specs=[smem, smem] + [vmem] * 17,
        out_specs=(vmem,) * 4,
        scratch_shapes=[
            pltpu.VMEM((16, B, B), BF),
            pltpu.VMEM((N_SLOT + 1, B, B), F32),
        ],
        compiler_params=pltpu.CompilerParams(vmem_limit_bytes=VMEM_LIMIT),
        cost_estimate=pl.CostEstimate(
            flops=128 * 2 * B**3, bytes_accessed=22 * 2**20, transcendentals=0
        ),
        name="tile_sums",
    )(words, count, tiles, *pieces)


def gather(block, chunk):
    near = lax.ppermute(block, "row", Y_HI)
    up = lax.ppermute(block, "row", X_UP)
    down = lax.ppermute(block, "row", X_DOWN)
    near_up = lax.ppermute(near, "row", X_UP)
    near_down = lax.ppermute(near, "row", X_DOWN)
    far = lax.ppermute(up, "row", X_UP)
    near_far = lax.ppermute(near_down, "row", X_DOWN)
    return [[block, near], [down, near_down], [far, near_far], [up, near_up]]


def add(*terms):
    total = terms[0].astype(F32)
    for term in terms[1:]:
        total = total + term.astype(F32)
    return total


def scatter_sum(keep, send):
    other = lax.ppermute(send, "col", CORE)
    far = add(keep[4:6], other[4:6]).astype(BF)
    from_low = lax.ppermute(far[0], "col", Z_UP)
    from_high = lax.ppermute(far[1], "col", Z_DOWN)
    up = jnp.stack([add(keep[2], other[2], from_low), add(keep[3], other[3])]).astype(BF)
    down = jnp.stack([add(keep[6], other[6]), add(keep[7], other[7], from_high)]).astype(BF)
    low = lax.ppermute(up, "col", Z_UP)
    high = lax.ppermute(down, "col", Z_DOWN)
    out = add(keep[1], other[1], low[1], high[1]).astype(BF)
    mine = add(keep[0], other[0], low[0], high[0])
    return mine, lax.ppermute(out, "col", Y_LO)


def per_device(features, inject, weight, tiles, tile_rows, tile_cols, tile_count, flags):
    count = tile_count[0]
    words = tile_words(tile_rows[0, 0], tile_cols[0, 0], count)
    tile_set = tiles[0, 0]
    blocks = [features[:B], features[B:]]
    previous = blocks
    for step in range(ITERS):
        previous = blocks
        parts = [gather(blocks[k], k) for k in range(2)]
        pieces = [parts[k][dx][dy] for dx in range(4) for dy in range(2) for k in range(2)]
        sums = tile_sums(words, count, tile_set, pieces)
        updated = []
        for k in range(2):
            mine, other = scatter_sum(sums[2 * k], sums[2 * k + 1])
            aggregate = add(mine, other).astype(BF)
            pre = jnp.dot(aggregate, weight, preferred_element_type=F32)
            pre = pre + inject[k * B : (k + 1) * B].astype(F32)
            updated.append(jnp.where(flags[k] == 1, blocks[k], jnp.tanh(pre).astype(BF)))
        blocks = updated
    change = [b.astype(F32) - p.astype(F32) for b, p in zip(blocks, previous)]
    residual = jnp.stack([jnp.sum(c * c) for c in change])
    return jnp.concatenate(blocks, axis=0), residual


def solution(mesh):
    in_specs = (
        P(("row", "col"), None),
        P(("row", "col"), None),
        P(),
        P("row", "col", None, None, None),
        P("row", "col", None),
        P("row", "col", None),
        P("row", "col"),
        P(("row", "col")),
    )
    out_specs = (P(("row", "col"), None), P(("row", "col")))
    return jax.shard_map(
        per_device, mesh=mesh, in_specs=in_specs, out_specs=out_specs, check_vma=False
    )
```

```python
import functools

import jax
import jax.numpy as jnp
from jax import lax
from jax.experimental import pallas as pl
from jax.experimental.pallas import tpu as pltpu
from jax.sharding import PartitionSpec as P

ITERS = 2
B = 256
BF = jnp.bfloat16
F32 = jnp.float32
N_SLOT = 32
N_EARLY = 10
GROUP = 16
VMEM_LIMIT = 16 * 2**20
PIECES = 0x53726410


def col_perm(f):
    pairs = []
    for i in range(16):
        y, z, c = f(i // 8, i // 2 % 4, i % 2)
        pairs.append((i, (y % 2) * 8 + (z % 4) * 2 + c % 2))
    return pairs


def row_perm(f):
    pairs = []
    for i in range(8):
        x, y = f(i // 2, i % 2)
        pairs.append((i, (x % 4) * 2 + y % 2))
    return pairs


CORE = col_perm(lambda y, z, c: (y, z, c + 1))
Z_UP = col_perm(lambda y, z, c: (y, z + 1, c))
Z_DOWN = col_perm(lambda y, z, c: (y, z - 1, c))
Y_LO = col_perm(lambda y, z, c: (y + 1, z, c))
Y_HI = row_perm(lambda x, y: (x, y + 1))
X_UP = row_perm(lambda x, y: (x + 1, y))
X_DOWN = row_perm(lambda x, y: (x - 1, y))
X_FAR = row_perm(lambda x, y: (x + 2, y))


SMEM = pl.BlockSpec(memory_space=pltpu.SMEM)
VMEM = pl.BlockSpec(memory_space=pltpu.VMEM)
HBM = pl.BlockSpec(memory_space=pltpu.HBM)
PARAMS = pltpu.CompilerParams(vmem_limit_bytes=VMEM_LIMIT)


def cost(n_tiles, extra):
    return pl.CostEstimate(
        flops=n_tiles * 2 * B**3, bytes_accessed=extra, transcendentals=0
    )


def tile_words(rows, cols, count):
    row, col = lax.axis_index("row"), lax.axis_index("col")
    x, yh = row >> 1, row & 1
    yl, z, core = col >> 3, (col >> 1) & 3, col & 1
    half = ((rows >> 1) & 1) ^ core
    dst = (rows & 1) * 16 + half * 8 + (((rows >> 2) - z) & 3) * 2 + ((rows >> 4) ^ yl)
    place = (((cols >> 2) - x) & 3) * 2 + (((cols >> 1) & 1) ^ yh)
    src = ((PIECES >> (place * 4)) & 15) * 2 + (cols & 1)
    index = jnp.arange(rows.shape[0], dtype=jnp.int32)
    live = index < count
    early = live & (src < N_EARLY)
    word = index + src * 256 + dst * 65536
    key = jnp.where(early, 0, jnp.where(live, 1, 2)) * 256 + index
    rank = jnp.sum((key[None, :] < key[:, None]).astype(jnp.int32), axis=1)
    words = jnp.sum(jnp.where(rank[:, None] == index[None, :], word[:, None], 0), axis=0)
    return words, jnp.stack([jnp.sum(early.astype(jnp.int32)), count[0]])


def copy_kernel(source, target, sem):
    copy = pltpu.make_async_copy(source, target, sem)
    copy.start()
    copy.wait()


def copy_in(value):
    return pl.pallas_call(
        copy_kernel,
        out_shape=jax.ShapeDtypeStruct(value.shape, value.dtype),
        in_specs=[HBM],
        out_specs=VMEM,
        scratch_shapes=[pltpu.SemaphoreType.DMA],
        compiler_params=PARAMS,
        name="copy_in",
    )(value)


def add_tiles(words, start, stop, unroll, first, held, state, acc, arrive=None):
    last = held.shape[0] - 1

    @pl.loop(0, (stop - start + unroll - 1) // unroll)
    def _(i):
        if arrive is not None:
            arrive(i)
        for u in range(unroll):
            at = start + i * unroll + u
            here = jnp.minimum(at, last)
            word = words[here]
            dst = jnp.where(at < stop, word >> 16, N_SLOT)
            src = jnp.clip(((word >> 8) & 255) - first, 0, state.shape[0] - 1)
            acc[dst] += jnp.dot(held[here], state[src], preferred_element_type=F32)


def load_state(pieces, state):
    for p, piece in enumerate(pieces):
        state[2 * p] = piece[:B]
        state[2 * p + 1] = piece[B:]


def fetch_kernel(words, sizes, tiles, *refs):
    pieces, (acc, held, state, sem) = refs[:5], refs[5:]
    groups = (sizes[1] + GROUP - 1) // GROUP
    early_groups = (sizes[0] + GROUP - 1) // GROUP
    ahead = 4

    def fetch(i):
        for u in range(GROUP):
            at = i * GROUP + u
            pltpu.make_async_copy(tiles.at[words[at] & 255], held.at[at], sem.at[i]).start()

    def arrive(i):
        here = held.at[pl.ds(i * GROUP, GROUP)]
        pltpu.make_async_copy(tiles.at[pl.ds(0, GROUP)], here, sem.at[i]).wait()

    def step(i):
        @pl.when(i + ahead < groups)
        def _():
            fetch(i + ahead)

        arrive(i)

    @pl.loop(0, jnp.minimum(groups, ahead))
    def _(i):
        fetch(i)

    acc[...] = jnp.zeros_like(acc)
    load_state(pieces, state)
    add_tiles(words, 0, sizes[0], GROUP, 0, held, state, acc, step)

    @pl.loop(early_groups, groups)
    def _(i):
        step(i)


def early_kernel(words, sizes, held, *refs):
    pieces, (acc, state) = refs[:5], refs[5:]
    acc[...] = jnp.zeros_like(acc)
    load_state(pieces, state)
    add_tiles(words, 0, sizes[0], GROUP, 0, held, state, acc)


def late_kernel(words, sizes, held, acc, *refs):
    pieces, outs, state = refs[:3], refs[3:7], refs[8]
    load_state(pieces, state)
    add_tiles(words, sizes[0], sizes[1], 8, N_EARLY, held, state, acc)
    for i, out in enumerate(outs):
        for s in range(8):
            out[s] = acc[i * 8 + s].astype(BF)


def tile_sums(words, sizes, tiles, held, early, late):
    acc_type = jax.ShapeDtypeStruct((N_SLOT + 1, B, B), F32)
    n_tiles = tiles.shape[0]
    if held is None:
        acc, held = pl.pallas_call(
            fetch_kernel,
            out_shape=(acc_type, jax.ShapeDtypeStruct(tiles.shape, BF)),
            in_specs=[SMEM, SMEM, HBM] + [VMEM] * len(early),
            out_specs=(VMEM, VMEM),
            scratch_shapes=[
                pltpu.VMEM((N_EARLY, B, B), BF),
                pltpu.SemaphoreType.DMA((n_tiles // GROUP,)),
            ],
            compiler_params=PARAMS,
            cost_estimate=cost(80, 0),
            name="fetch_tiles",
        )(words, sizes, tiles, *early)
    else:
        acc = pl.pallas_call(
            early_kernel,
            out_shape=acc_type,
            in_specs=[SMEM, SMEM] + [VMEM] * (1 + len(early)),
            out_specs=VMEM,
            scratch_shapes=[pltpu.VMEM((N_EARLY, B, B), BF)],
            compiler_params=PARAMS,
            cost_estimate=cost(80, 0),
            name="early_tiles",
        )(words, sizes, held, *early)
    out = jax.ShapeDtypeStruct((8, B, B), BF)
    sums = pl.pallas_call(
        late_kernel,
        out_shape=(out,) * 4 + (acc_type,),
        in_specs=[SMEM, SMEM] + [VMEM] * (2 + len(late)),
        out_specs=(VMEM,) * 5,
        scratch_shapes=[pltpu.VMEM((16 - N_EARLY, B, B), BF)],
        input_output_aliases={3: 4},
        compiler_params=PARAMS,
        cost_estimate=cost(48, 0),
        name="late_tiles",
    )(words, sizes, held, acc, *late)[:4]
    return sums, held


def gather(state):
    far = lax.ppermute(state, "row", X_FAR)
    near = lax.ppermute(state, "row", Y_HI)
    up = lax.ppermute(state, "row", X_UP)
    down = lax.ppermute(state, "row", X_DOWN)
    near_up = lax.ppermute(near, "row", X_UP)
    near_down = lax.ppermute(near, "row", X_DOWN)
    near_far = lax.ppermute(far, "row", Y_HI)
    return (state, near, far, up, down), (near_up, near_down, near_far)


def add(*terms):
    total = terms[0].astype(F32)
    for term in terms[1:]:
        total = total + term.astype(F32)
    return total


def scatter_sum(keep, send):
    other = lax.ppermute(send, "col", CORE)
    far = add(keep[4:6], other[4:6]).astype(BF)
    from_low = lax.ppermute(far[0], "col", Z_UP)
    from_high = lax.ppermute(far[1], "col", Z_DOWN)
    up = jnp.stack([add(keep[2], other[2], from_low), add(keep[3], other[3])]).astype(BF)
    down = jnp.stack([add(keep[6], other[6]), add(keep[7], other[7], from_high)]).astype(BF)
    low = lax.ppermute(up, "col", Z_UP)
    high = lax.ppermute(down, "col", Z_DOWN)
    out = add(keep[1], other[1], low[1], high[1]).astype(BF)
    return keep, other, low, high, lax.ppermute(out, "col", Y_LO)


def update_kernel(flags, weight, inject, state, *refs):
    terms, (new, residual) = refs[:10], refs[10:]
    for k in range(2):
        keep, other, low, high, across = terms[5 * k : 5 * k + 5]
        total = add(keep[0], other[0], low[0], high[0], across[...])
        pre = jnp.dot(total.astype(BF), weight[...], preferred_element_type=F32)
        rows = pl.ds(k * B, B)
        old = state[rows]
        updated = jnp.tanh(pre + inject[rows].astype(F32)).astype(BF)
        updated = jnp.where(flags[k] == 1, old, updated)
        new[rows] = updated
        change = updated.astype(F32) - old.astype(F32)
        residual[k] = jnp.sum(change * change)


def update(flags, weight, inject, state, terms):
    return pl.pallas_call(
        update_kernel,
        out_shape=(
            jax.ShapeDtypeStruct(state.shape, BF),
            jax.ShapeDtypeStruct((2,), F32),
        ),
        in_specs=[SMEM] + [VMEM] * 13,
        out_specs=(VMEM, SMEM),
        compiler_params=PARAMS,
        cost_estimate=cost(2, 0),
        name="update",
    )(flags, weight, inject, state, *terms)


def per_device(features, inject, weight, tiles, tile_rows, tile_cols, tile_count, flags):
    words, sizes = tile_words(tile_rows[0, 0], tile_cols[0, 0], tile_count[0])
    tile_set = pltpu.with_memory_space_constraint(tiles[0, 0], pltpu.HBM)
    state = copy_in(pltpu.with_memory_space_constraint(features, pltpu.HBM))
    held = None
    for step in range(ITERS):
        early, late = gather(state)
        sums, held = tile_sums(words, sizes, tile_set, held, early, late)
        terms = scatter_sum(sums[0], sums[1]) + scatter_sum(sums[2], sums[3])
        state, residual = update(flags, weight, inject, state, terms)
    return state, residual


def solution(mesh):
    in_specs = (
        P(("row", "col"), None),
        P(("row", "col"), None),
        P(),
        P("row", "col", None, None, None),
        P("row", "col", None),
        P("row", "col", None),
        P("row", "col"),
        P(("row", "col")),
    )
    out_specs = (P(("row", "col"), None), P(("row", "col")))
    return jax.shard_map(
        per_device, mesh=mesh, in_specs=in_specs, out_specs=out_specs, check_vma=False
    )
```

```python
import functools

import jax
import jax.numpy as jnp
from jax import lax
from jax.experimental import pallas as pl
from jax.experimental.pallas import tpu as pltpu
from jax.sharding import PartitionSpec as P

ITERS = 2
B = 256
BF = jnp.bfloat16
F32 = jnp.float32
N_SLOT = 32
FIRST = (0, 6, 10, 16)
GROUP = 16
VMEM_LIMIT = 16 * 2**20
PIECES = (0, 1, 4, 6, 2, 7, 3, 5)


def col_perm(f):
    pairs = []
    for i in range(16):
        y, z, c = f(i // 8, i // 2 % 4, i % 2)
        pairs.append((i, (y % 2) * 8 + (z % 4) * 2 + c % 2))
    return pairs


def row_perm(f):
    pairs = []
    for i in range(8):
        x, y = f(i // 2, i % 2)
        pairs.append((i, (x % 4) * 2 + y % 2))
    return pairs


CORE = col_perm(lambda y, z, c: (y, z, c + 1))
Z_UP = col_perm(lambda y, z, c: (y, z + 1, c))
Z_DOWN = col_perm(lambda y, z, c: (y, z - 1, c))
Z_FAR = col_perm(lambda y, z, c: (y, z + 2, c))
Y_LO = col_perm(lambda y, z, c: (y + 1, z, c))
Y_HI = row_perm(lambda x, y: (x, y + 1))
X_UP = row_perm(lambda x, y: (x + 1, y))
X_DOWN = row_perm(lambda x, y: (x - 1, y))
X_FAR = row_perm(lambda x, y: (x + 2, y))


SMEM = pl.BlockSpec(memory_space=pltpu.SMEM)
VMEM = pl.BlockSpec(memory_space=pltpu.VMEM)
HBM = pl.BlockSpec(memory_space=pltpu.HBM)
PARAMS = pltpu.CompilerParams(vmem_limit_bytes=VMEM_LIMIT)


def cost(n_tiles, extra):
    return pl.CostEstimate(
        flops=n_tiles * 2 * B**3, bytes_accessed=extra, transcendentals=0
    )


def prepare_kernel(row_list, col_list, count, features, table, state, rows, cols, sem):
    copies = [
        pltpu.make_async_copy(source, target, sem.at[s])
        for s, (source, target) in enumerate(
            ((row_list, rows), (col_list, cols), (features, state))
        )
    ]
    for copy in copies:
        copy.start()
    copies[0].wait()
    copies[1].wait()
    row, col = lax.axis_index("row"), lax.axis_index("col")
    x, yh = row >> 1, row & 1
    yl, z, core = col >> 3, (col >> 1) & 3, col & 1
    n = rows.shape[1]
    i, j = rows[...], cols[...]
    dy = (i >> 4) ^ yl
    half = ((i >> 1) & 1) ^ core
    dst = dy * 16 + half * 8 + (((i >> 2) - z) & 3) * 2 + (i & 1)
    place = (((j >> 2) - x) & 3) * 2 + (((j >> 1) & 1) ^ yh)
    src = jnp.zeros_like(place)
    for at, piece in enumerate(PIECES):
        src = jnp.where(place == at, piece, src)
    src = src * 2 + (j & 1)
    index = lax.broadcasted_iota(jnp.int32, (1, n), 1)
    kind = jnp.where(src < FIRST[1], 0, jnp.where(src < FIRST[2], 1, 3 - dy))
    kind = jnp.where(index < count[0], kind, 4)
    word = index + src * 256 + dst * 65536
    key = jnp.broadcast_to((kind * 256 + index).astype(F32), (n, n))
    rank = jnp.sum((key < key.T).astype(F32), axis=1, keepdims=True)
    slot = lax.broadcasted_iota(jnp.int32, (n, n), 1).astype(F32)
    listed = jnp.broadcast_to(word.astype(F32), (n, n)).T
    words = jnp.sum(jnp.where(rank == slot, listed, 0.0), axis=0, keepdims=True)
    ends = jnp.zeros((1, n), F32)
    for k in range(4):
        end = jnp.sum((kind <= k).astype(F32), axis=1, keepdims=True)
        ends = jnp.where(index == k, end, ends)
    table[0:1, :] = words.astype(jnp.int32)
    table[1:2, :] = ends.astype(jnp.int32)
    copies[2].wait()


def prepare(rows, cols, count, features):
    return pl.pallas_call(
        prepare_kernel,
        out_shape=(
            jax.ShapeDtypeStruct((2, rows.shape[1]), jnp.int32),
            jax.ShapeDtypeStruct(features.shape, features.dtype),
        ),
        in_specs=[HBM, HBM, SMEM, HBM],
        out_specs=(VMEM, VMEM),
        scratch_shapes=[pltpu.VMEM(rows.shape, jnp.int32)] * 2 + [pltpu.SemaphoreType.DMA((3,))],
        compiler_params=PARAMS,
        cost_estimate=cost(0, 0),
        name="prepare",
    )(rows, cols, count, features)


def add_tiles(table, start, stop, unroll, first, held, state, acc, arrive=None):
    last = held.shape[0] - 1

    @pl.loop(0, (stop - start + unroll - 1) // unroll)
    def _(i):
        if arrive is not None:
            arrive(i)
        for u in range(unroll):
            at = start + i * unroll + u
            here = jnp.minimum(at, last)
            word = table[0, here]
            dst = jnp.where(at < stop, word >> 16, N_SLOT)
            src = jnp.clip(((word >> 8) & 255) - first, 0, state.shape[0] - 1)
            acc[dst] += jnp.dot(held[here], state[src], preferred_element_type=F32)


def load_state(pieces, state):
    for p, piece in enumerate(pieces):
        state[2 * p] = piece[:B]
        state[2 * p + 1] = piece[B:]


def fetch_kernel(table, tiles, *refs):
    pieces, (acc, held, state, sem) = refs[:3], refs[3:]
    groups = (table[1, 3] + GROUP - 1) // GROUP
    first_groups = (table[1, 0] + GROUP - 1) // GROUP
    ahead = 4

    def fetch(i):
        for u in range(GROUP):
            at = i * GROUP + u
            pltpu.make_async_copy(tiles.at[table[0, at] & 255], held.at[at], sem.at[i]).start()

    def step(i):
        @pl.when(i + ahead < groups)
        def _():
            fetch(i + ahead)

        here = held.at[pl.ds(i * GROUP, GROUP)]
        pltpu.make_async_copy(tiles.at[pl.ds(0, GROUP)], here, sem.at[i]).wait()

    @pl.loop(0, jnp.minimum(groups, ahead))
    def _(i):
        fetch(i)

    acc[...] = jnp.zeros_like(acc)
    load_state(pieces, state)
    add_tiles(table, 0, table[1, 0], GROUP, FIRST[0], held, state, acc, step)

    @pl.loop(first_groups, groups)
    def _(i):
        step(i)


def first_kernel(table, held, *refs):
    pieces, (acc, state) = refs[:3], refs[3:]
    acc[...] = jnp.zeros_like(acc)
    load_state(pieces, state)
    add_tiles(table, 0, table[1, 0], GROUP, FIRST[0], held, state, acc)


def second_kernel(table, held, acc, *refs):
    pieces, state = refs[:2], refs[3]
    load_state(pieces, state)
    add_tiles(table, table[1, 0], table[1, 1], 8, FIRST[1], held, state, acc)


def late_kernel(dy, table, held, acc, *refs):
    pieces, outs, state = refs[:3], refs[3:5], refs[6]
    load_state(pieces, state)
    start, stop = table[1, 2 - dy], table[1, 3 - dy]
    add_tiles(table, start, stop, 8, FIRST[2], held, state, acc)
    for half, out in enumerate(outs):
        for s in range(8):
            out[s] = acc[dy * 16 + half * 8 + s].astype(BF)


def tile_sums(table, tiles, held, first, second, late):
    acc_type = jax.ShapeDtypeStruct((N_SLOT + 1, B, B), F32)
    n_tiles = tiles.shape[0]
    blocks = [pltpu.VMEM((stop - start, B, B), BF) for start, stop in zip(FIRST, FIRST[1:])]
    if held is None:
        acc, held = pl.pallas_call(
            fetch_kernel,
            out_shape=(acc_type, jax.ShapeDtypeStruct(tiles.shape, BF)),
            in_specs=[SMEM, HBM] + [VMEM] * len(first),
            out_specs=(VMEM, VMEM),
            scratch_shapes=[blocks[0], pltpu.SemaphoreType.DMA((n_tiles // GROUP,))],
            compiler_params=PARAMS,
            cost_estimate=cost(100, 0),
            name="fetch_tiles",
        )(table, tiles, *first)
    else:
        acc = pl.pallas_call(
            first_kernel,
            out_shape=acc_type,
            in_specs=[SMEM] + [VMEM] * (1 + len(first)),
            out_specs=VMEM,
            scratch_shapes=[blocks[0]],
            compiler_params=PARAMS,
            cost_estimate=cost(50, 0),
            name="first_tiles",
        )(table, held, *first)
    acc = pl.pallas_call(
        second_kernel,
        out_shape=acc_type,
        in_specs=[SMEM] + [VMEM] * (2 + len(second)),
        out_specs=VMEM,
        scratch_shapes=[blocks[1]],
        input_output_aliases={2: 0},
        compiler_params=PARAMS,
        cost_estimate=cost(50, 0),
        name="second_tiles",
    )(table, held, acc, *second)
    out = jax.ShapeDtypeStruct((8, B, B), BF)
    sums = []
    for dy in (1, 0):
        keep, send, acc = pl.pallas_call(
            functools.partial(late_kernel, dy),
            out_shape=(out, out, acc_type),
            in_specs=[SMEM] + [VMEM] * (2 + len(late)),
            out_specs=(VMEM,) * 3,
            scratch_shapes=[blocks[2]],
            input_output_aliases={2: 2},
            compiler_params=PARAMS,
            cost_estimate=cost(160, 0),
            name=f"late_tiles_{dy}",
        )(table, held, acc, *late)
        sums = [keep, send] + sums
    return sums, held


def gather(state):
    far = lax.ppermute(state, "row", X_FAR)
    near = lax.ppermute(state, "row", Y_HI)
    up = lax.ppermute(state, "row", X_UP)
    down = lax.ppermute(state, "row", X_DOWN)
    near_up = lax.ppermute(near, "row", X_UP)
    near_down = lax.ppermute(near, "row", X_DOWN)
    near_far = lax.ppermute(far, "row", Y_HI)
    return (state, near, far), (up, down), (near_up, near_down, near_far)


def add(*terms):
    total = terms[0].astype(F32)
    for term in terms[1:]:
        total = total + term.astype(F32)
    return total


def add_kernel(*refs):
    terms, out = refs[:-1], refs[-1]
    for k in range(2):
        out[k] = add(*(term[k] for term in terms)).astype(out.dtype)


def add_blocks(dtype, claim, *terms):
    return pl.pallas_call(
        add_kernel,
        out_shape=jax.ShapeDtypeStruct((2, B, B), dtype),
        in_specs=[VMEM] * len(terms),
        out_specs=VMEM,
        compiler_params=PARAMS,
        cost_estimate=cost(claim, 0),
        name="add_blocks",
    )(*terms)


def col_sum(keep_0, send_0, keep_1, send_1):
    other_1 = lax.ppermute(send_1, "col", CORE)
    other_0 = lax.ppermute(send_0, "col", CORE)
    far_1 = add(keep_1[4:6], other_1[4:6]).astype(BF)
    across_far = lax.ppermute(far_1, "col", Y_LO)
    low_1 = lax.ppermute(add(keep_1[2:4], other_1[2:4]).astype(BF), "col", Z_UP)
    high_1 = lax.ppermute(add(keep_1[6:8], other_1[6:8]).astype(BF), "col", Z_DOWN)
    low_0 = lax.ppermute(add(keep_0[2:4], other_0[2:4]).astype(BF), "col", Z_UP)
    high_0 = lax.ppermute(add(keep_0[6:8], other_0[6:8]).astype(BF), "col", Z_DOWN)
    far_0 = add(keep_0[4:6], other_0[4:6])
    far = lax.ppermute(add_blocks(BF, 0, far_0, across_far), "col", Z_FAR)
    out = add_blocks(BF, 0, keep_1, other_1, low_1, high_1)
    across = lax.ppermute(out, "col", Y_LO)
    near = add_blocks(F32, 300, keep_0, other_0, low_0, high_0)
    return near, far, across


def update_kernel(flags, weight, inject, state, *refs):
    terms, (new, residual) = refs[:3], refs[3:]
    for k in range(2):
        total = add(*(term[k] for term in terms))
        pre = jnp.dot(total.astype(BF), weight[...], preferred_element_type=F32)
        rows = pl.ds(k * B, B)
        old = state[rows]
        updated = jnp.tanh(pre + inject[rows].astype(F32)).astype(BF)
        updated = jnp.where(flags[k] == 1, old, updated)
        new[rows] = updated
        change = updated.astype(F32) - old.astype(F32)
        residual[k] = jnp.sum(change * change)


def update(flags, weight, inject, state, terms):
    return pl.pallas_call(
        update_kernel,
        out_shape=(
            jax.ShapeDtypeStruct(state.shape, BF),
            jax.ShapeDtypeStruct((2,), F32),
        ),
        in_specs=[SMEM] + [VMEM] * 6,
        out_specs=(VMEM, SMEM),
        compiler_params=PARAMS,
        cost_estimate=cost(2, 0),
        name="update",
    )(flags, weight, inject, state, *terms)


def per_device(features, inject, weight, tiles, tile_rows, tile_cols, tile_count, flags):
    tile_set = pltpu.with_memory_space_constraint(tiles[0, 0], pltpu.HBM)
    in_hbm = [
        pltpu.with_memory_space_constraint(value, pltpu.HBM)
        for value in (tile_rows[0], tile_cols[0], features)
    ]
    table, state = prepare(in_hbm[0], in_hbm[1], tile_count[0], in_hbm[2])
    held = None
    for step in range(ITERS):
        sums, held = tile_sums(table, tile_set, held, *gather(state))
        state, residual = update(flags, weight, inject, state, col_sum(*sums))
    return state, residual


def solution(mesh):
    in_specs = (
        P(("row", "col"), None),
        P(("row", "col"), None),
        P(),
        P("row", "col", None, None, None),
        P("row", "col", None),
        P("row", "col", None),
        P("row", "col"),
        P(("row", "col")),
    )
    out_specs = (P(("row", "col"), None), P(("row", "col")))
    return jax.shard_map(
        per_device, mesh=mesh, in_specs=in_specs, out_specs=out_specs, check_vma=False
    )
```
